32 devices in a mesh: sec: 8 (over y, x, core), span: 4 (over z).
Axes of the slice: x: 2, y: 2, z: 4, core: 2. Of those that a mesh axis runs over, the one named last changes fastest.
Arguments:
- density: float32 [192, 1024], P('sec', 'span'), may hold values from 0.5 to 2
- fields: float32 [4, 192, 1024], P(None, 'sec', 'span'), may hold values from -6 to 6
- bins: int32 [192, 1024], P('sec', 'span'), may hold values from 0 to 127
- owner: int32 [192], P('sec'), may hold values from 0 to 31
- species: float32 [32, 32, 128], P(('sec', 'span')), may hold values from -6 to 6
- rate_matrix: float32 [32, 32], replicated, may hold values from -1 to 1
- inv_weight: float32 [32], replicated, may hold values from 0.5 to 2
- formation: float32 [32], replicated, may hold values from -4 to 4
Outputs:
- species_out: float32 [32, 32, 128], P(('sec', 'span'))
- density_out: float32 [192, 1024], P('sec', 'span')
- fields_out: float32 [4, 192, 1024], P(None, 'sec', 'span')
The draws below stay inside these ranges and needn't reach their ends.
All inputs are finite; a program needn't handle non-finite values.
Results may differ from the reference program's by a relative error of at most 0.0003.
Values sent between devices are 32-bit elements; how exact they have to be, the bound alone decides.
A program may use at most 64 MiB of HBM per device.

```python
import math
import jax
import jax.numpy as jnp
import numpy as np
from jax import lax

BINS = 128
SPECIES = 32
COUPLING = 2
SECTIONS = 32
COLS = 192
ZSPAN = 1024


def touch_ends(values, stream_key, smallest, high):
    dims = values.shape
    index_at = [jax.random.randint(jax.random.fold_in(stream_key, axis), (), 0, dims[axis]) for axis in range(len(dims))]
    values = values.at[tuple(index_at)].set(smallest)
    longest = dims.index(max(dims))
    index_at[longest] = (index_at[longest] + 1) % dims[longest]
    return values.at[tuple(index_at)].set(high)


def levels(own_key, dims, split, least, top_value):
    loudness = 1.0
    for axis_at, blocks in split:
        steps = jax.random.uniform(jax.random.fold_in(jax.random.fold_in(own_key, 6), axis_at), (blocks,), jnp.float32, least / len(split), top_value / len(split))
        loudness = loudness * jnp.repeat(jnp.exp(steps), dims[axis_at] // blocks).reshape((-1,) + (1,) * (len(dims) - 1 - axis_at))
    return loudness


def cumulative_ranks(number_of, lean):
    portions = [(1 << 20) // math.isqrt(grade ** lean) + 1 for grade in range(1, number_of + 1)]
    scale = 1 + sum(portions) // (1 << 30)
    return np.cumsum(np.array([max(1, weight // scale) for weight in portions]))


def ranked(key, dims, number_of, skew):
    grid = cumulative_ranks(number_of, skew)
    ticket = jax.random.randint(jax.random.fold_in(key, 1), dims, 0, int(grid[number_of - 1]))
    grade = jnp.searchsorted(jnp.asarray(grid, jnp.int32), ticket, side="right")
    return jax.random.permutation(jax.random.fold_in(key, 2), number_of)[grade].astype(jnp.int32)


def bell_draw(key, shape, width, reach, shards=(), kind=jnp.bfloat16):
    drawn = width * jax.random.normal(key, shape, jnp.float32)
    if shards:
        drawn = drawn * levels(key, shape, shards, -0.22, 0.18)
    return jnp.clip(drawn, -reach, reach).astype(kind)


def setup_inputs(seed: int = 0) -> dict:
    keys = jax.random.split(jax.random.key(seed), 9)
    density = jnp.clip(jnp.exp(math.log(2.0) - 1.3862944 * jax.random.uniform(keys[0], (COLS, ZSPAN), jnp.float32) ** levels(keys[0], (COLS, ZSPAN), ((0, 8), (1, 4)), -0.2, 0.2)), 0.5, 2.0)
    fields = bell_draw(keys[1], (4, COLS, ZSPAN), 1.0, 6.0, ((1, 8), (2, 4)), jnp.float32)
    bins = touch_ends(ranked(keys[2], (COLS, ZSPAN), BINS, 2), jax.random.fold_in(keys[2], 3), 0, BINS - 1).astype(jnp.int32)
    owner = touch_ends(ranked(keys[3], (COLS,), SECTIONS, 2), jax.random.fold_in(keys[3], 3), 0, SECTIONS - 1).astype(jnp.int32)
    species = bell_draw(keys[4], (SECTIONS, SPECIES, BINS), 1.0, 6.0, ((0, 32),), jnp.float32)
    rate_matrix = bell_draw(keys[5], (SPECIES, SPECIES), SPECIES ** -0.5, 1.0, (), jnp.float32)
    inv_weight = jnp.clip(jnp.exp(jax.random.uniform(keys[6], (SPECIES,), jnp.float32, math.log(0.5), math.log(2.0))), 0.5, 2.0)
    formation = bell_draw(keys[7], (SPECIES,), 1.0, 4.0, (), jnp.float32)
    return dict(density=density, fields=fields, bins=bins, owner=owner, species=species, rate_matrix=rate_matrix, inv_weight=inv_weight, formation=formation)


def reference(density, fields, bins, owner, species, rate_matrix, inv_weight, formation):
    segment = (owner[:, None] * BINS + bins).reshape(-1)
    eta = (jnp.arange(BINS, dtype=jnp.float32) + 0.5) / BINS
    for step in range(COUPLING):
        values = [density] + [density * fields[k] for k in range(4)]
        sums = jnp.stack([jax.ops.segment_sum(v.reshape(-1), segment, num_segments=SECTIONS * BINS) for v in values])
        sums = sums.reshape(5, SECTIONS, BINS)
        weight = jnp.maximum(sums[0], 1.0)
        cond = sums[1:] / weight[None]
        temp = 1.0 + 4.0 * eta * (1.0 - eta) + 0.5 * jnp.tanh(cond[2])
        rate = jnp.exp(2.0 * (1.0 - 1.0 / temp))
        react = jnp.einsum('ij,sjb->sib', rate_matrix, species, precision=lax.Precision.HIGHEST) * rate[:, None, :]
        padded = jnp.pad(species, ((0, 0), (0, 0), (1, 1)))
        lap = padded[:, :, 2:] + padded[:, :, :-2] - 2.0 * species
        before = jnp.concatenate([jnp.zeros_like(species[:1]), species[:-1]], axis=0)
        mixing = 0.2 * jax.nn.sigmoid(cond[1])
        carry = 0.3 * jax.nn.sigmoid(cond[0])
        species = species + mixing[:, None, :] * lap - carry[:, None, :] * (species - before) + 0.2 * react
        mix = 1.0 + jnp.sum(inv_weight[None, :, None] * species * species, axis=1) / SPECIES
        rho_c = 1.0 / (temp * mix)
        temp_c = temp + 0.1 * jnp.sum(formation[None, :, None] * react, axis=1) - 0.2 * jax.nn.sigmoid(cond[3]) * (temp - 0.5)
        rho_cell = rho_c.reshape(-1)[segment].reshape(density.shape)
        temp_cell = temp_c.reshape(-1)[segment].reshape(density.shape)
        lapz = jnp.roll(fields, 1, axis=2) + jnp.roll(fields, -1, axis=2) - 2.0 * fields
        fields = fields + 0.2 * lapz
        fields = fields.at[2].add(0.3 * (temp_cell - fields[2]))
        density = rho_cell
    return species, density, fields
```

```python
import functools

import jax
import jax.numpy as jnp
from jax import lax
from jax.experimental import pallas as pl
from jax.experimental.pallas import tpu as pltpu
from jax.sharding import PartitionSpec as P

MESH = pl.DeviceIdType.MESH
F32 = jnp.float32
BF16 = jnp.bfloat16
HIGH = lax.Precision.HIGHEST
NQ = 10
ROWS = 3


def split(x):
    hi = x.astype(BF16)
    return hi, (x - hi.astype(F32)).astype(BF16)


def iota(shape, dim):
    return lax.broadcasted_iota(jnp.int32, shape, dim)


def shifted(x, left, right):
    width = x.shape[1]
    lane = iota(x.shape, 1)
    down = jnp.where(lane == 0, left, pltpu.roll(x, 1, 1))
    up = jnp.where(lane == width - 1, right, pltpu.roll(x, width - 1, 1))
    return down, up


def lap_bins(x):
    down, up = shifted(x, 0.0, 0.0)
    return up + down - 2.0 * x


def kernel(
    n, J, PK,
    owner, invw, form, density, fields, bins, species, rate_m,
    sp_out, den_out, f_out,
    halo_out, halo_in, spin, vals, hist, send1, in1, sum1, send2, in2, sendp, inp, prevs,
    table, tabc,
    hsend, hrecv, ssend, srecv, send1s, recv1s, send2s, recv2s, sendps, recvps, tsend, trecv,
):
    C, Z = density.shape
    K, B = species.shape[1], species.shape[2]
    N = n * J
    i, j = lax.axis_index("sec"), lax.axis_index("span")
    s = i * J + j

    def dev(t):
        return (lax.div(t, J), lax.rem(t, J))

    barrier = pltpu.get_barrier_semaphore()

    @pl.loop(1, N)
    def _(d):
        pl.semaphore_signal(barrier, inc=1, device_id=dev(lax.rem(s + d, N)), device_id_type=MESH)

    lane = iota((C, 128), 1)
    binf = bins[...].astype(F32)
    first, last = binf[:, :128], binf[:, Z - 128:]
    to_left = jnp.where(lane == 8, pltpu.roll(first, 8, 1), 0.0)
    to_right = jnp.where(lane == 8, pltpu.roll(last, 9, 1), 0.0)
    for k in range(4):
        here = (lane == 2 * k) | (lane == 2 * k + 1)
        head, tail = fields[k, :, :128], fields[k, :, Z - 128:]
        if k:
            head = pltpu.roll(head, 2 * k, 1)
        to_left = jnp.where(here, head, to_left)
        to_right = jnp.where(here, pltpu.roll(tail, 2 * k + 2, 1), to_right)
    halo_out[0] = to_left
    halo_out[1] = to_right

    pl.semaphore_wait(barrier, N - 1)

    copies = []
    for side, step in ((0, J - 1), (1, 1)):
        copies.append(pltpu.make_async_remote_copy(
            halo_out.at[side], halo_in.at[side], hsend.at[side], hrecv.at[side],
            device_id=(i, lax.rem(j + step, J)), device_id_type=MESH))
    for step in (1, 2):
        copies.append(pltpu.make_async_remote_copy(
            species.at[0], spin.at[step - 1], ssend.at[step - 1], srecv.at[step - 1],
            device_id=dev(lax.rem(s + step, N)), device_id_type=MESH))
    for c in copies:
        c.start()

    den = density[...]

    def put(k, x):
        for h in range(Z // 128):
            vals[h, k * C:(k + 1) * C, :] = x[:, h * 128:(h + 1) * 128]

    put(0, den)
    put(5, jnp.ones((C, Z), F32))
    for k in range(4):
        f = fields[k]
        put(1 + k, den * f)
        down, up = shifted(f, 0.0, 0.0)
        put(6 + k, f + 0.2 * (down + up - 2.0 * f))
    for k in range(NQ, 16):
        put(k, jnp.zeros((C, Z), F32))

    bin_id = iota((B, Z), 0)
    for c in range(C):
        hot = jnp.where(bin_id == bins[c:c + 1, :], 1.0, 0.0).astype(BF16)
        v = jnp.concatenate([vals[h, pl.ds(c, 16, stride=C), :] for h in range(Z // 128)], axis=1)
        hi, lo = split(v)
        both = jnp.concatenate([hi, lo], axis=0)
        r = lax.dot_general(both, hot, (((1,), (1,)), ((), ())), preferred_element_type=F32)
        hist[c * 16:(c + 1) * 16, :] = r[:16] + r[16:]

    RT = PK * J
    R, PC = n * RT, PK * C
    G = -(-NQ // PK)
    q = iota((1, PC), 1)
    qc = lax.rem(q, C)
    own_lane = jnp.zeros((1, PC), jnp.int32)
    for c in range(C):
        own_lane = jnp.where(qc == c, owner[c], own_lane)
    r = iota((R, PC), 0)
    rem = lax.rem(r, RT)
    sec = lax.div(r, RT) * J + lax.rem(rem, J)
    same = lax.div(rem, J) == lax.div(iota((R, PC), 1), C)
    place = jnp.where(same & (sec == own_lane), 1.0, 0.0).astype(BF16)

    for c in copies[:2]:
        c.wait()
    from_left, from_right = halo_in[1], halo_in[0]
    lanes_b = iota((C, B), 1)
    bin_first, bin_last = bins[:, 0:1], bins[:, Z - 1:Z]
    hot_first = jnp.where(lanes_b == bin_first, 0.2, 0.0)
    hot_last = jnp.where(lanes_b == bin_last, 0.2, 0.0)

    def edge(tile, at):
        return tile[:, at:at + 1]

    slabs = []
    for k in range(G * PK):
        h = hist[pl.ds(k, C, stride=16), :]
        if 6 <= k < NQ:
            h = (h + hot_first * edge(from_left, 2 * (k - 6) + 1)
                 + hot_last * edge(from_right, 2 * (k - 6)))
        slabs.append(h)
    groups = []
    for g in range(G):
        part = slabs[g * PK:(g + 1) * PK]
        groups.append(part[0] if PK == 1 else jnp.concatenate(part, axis=0))
    wide = jnp.concatenate(groups, axis=1)
    hi, lo = split(wide)
    binned = (jnp.dot(place, hi, preferred_element_type=F32)
              + jnp.dot(place, lo, preferred_element_type=F32))
    for t in range(n):
        for g in range(G):
            send1[t, g * RT:(g + 1) * RT, :] = binned[t * RT:(t + 1) * RT, g * 128:(g + 1) * 128]

    outs1 = []
    for d in range(1, n):
        t = lax.rem(i + d, n)
        outs1.append(pltpu.make_async_remote_copy(
            send1.at[t], in1.at[d - 1], send1s, recv1s, device_id=(t, j), device_id_type=MESH))
    for c in outs1:
        c.start()

    for c in copies[2:]:
        c.wait()
    row = iota((K, B), 0)
    wcol = jnp.zeros((K, B), F32)
    fcol = jnp.zeros((K, B), F32)
    for k in range(K):
        wcol = jnp.where(row == k, invw[k], wcol)
        fcol = jnp.where(row == k, form[k], fcol)
    cur = species[0]
    prev = jnp.where(s >= 1, spin[0], 0.0)
    prev2 = jnp.where(s >= 2, spin[1], 0.0)
    rm = rate_m[...]
    rc = jnp.dot(rm, cur, precision=HIGH, preferred_element_type=F32)
    rp = jnp.dot(rm, prev, precision=HIGH, preferred_element_type=F32)
    rrc = jnp.dot(rm, rc, precision=HIGH, preferred_element_type=F32)
    lap_c, lap_p, lap_rc = lap_bins(cur), lap_bins(prev), lap_bins(rc)
    frc = jnp.sum(fcol * rc, axis=0, keepdims=True)

    lane256 = iota((C, Z), 1)
    ahead = []
    ends = []
    for k in range(4):
        f = fields[k]
        l2, l1 = edge(from_left, 2 * k), edge(from_left, 2 * k + 1)
        r1, r2 = edge(from_right, 2 * k), edge(from_right, 2 * k + 1)
        down, up = shifted(f, l1, r1)
        a = f + 0.2 * (down + up - 2.0 * f)
        al = l1 + 0.2 * (l2 + f[:, 0:1] - 2.0 * l1)
        ar = r1 + 0.2 * (r2 + f[:, Z - 1:Z] - 2.0 * r1)
        ahead.append(a)
        ends.append((al, ar))
        if k != 2:
            down, up = shifted(a, al, ar)
            f_out[k] = a + 0.2 * (down + up - 2.0 * a)

    pltpu.make_async_copy(in1, in1, recv1s).wait()
    total = send1[i]
    for d in range(n - 1):
        total = total + in1[d]
    sum1[...] = total
    for t in range(J):
        send2[t, 0:NQ, :] = sum1[pl.ds(t, NQ, stride=J), :]
        if t:
            send2[t, NQ:NQ + 5, :] = sum1[pl.ds(t - 1, 5, stride=J), :]
        else:
            send2[t, NQ:NQ + 5, :] = jnp.zeros((5, B), F32)
        send2[t, NQ + 5:16, :] = jnp.zeros((1, B), F32)
    sendp[0:5, :] = sum1[pl.ds(J - 1, 5, stride=J), :]
    sendp[5:8, :] = jnp.zeros((3, B), F32)
    outp = pltpu.make_async_remote_copy(
        sendp, inp.at[j], sendps, recvps, device_id=(lax.rem(i + 1, n), 0), device_id_type=MESH)
    outs2 = []
    for d in range(1, J):
        t = lax.rem(j + d, J)
        outs2.append(pltpu.make_async_remote_copy(
            send2.at[t], in2.at[d - 1], send2s, recv2s, device_id=(i, t), device_id_type=MESH))
    outp.start()
    for c in outs2:
        c.start()

    pltpu.make_async_copy(in2, in2, recv2s).wait()
    total = send2[j]
    for d in range(J - 1):
        total = total + in2[d]
    prevs[0:5, :] = total[NQ:NQ + 5]

    @pl.when(j == 0)
    def _():
        pltpu.make_async_copy(inp, inp, recvps).wait()
        tp = inp[0]
        for d in range(1, J):
            tp = tp + inp[d]
        prevs[...] = tp

    before_sums = prevs[...]
    eta = (iota((1, B), 1).astype(F32) + 0.5) / B
    base = 1.0 + 4.0 * eta * (1.0 - eta)

    def sigmoid(x):
        return 1.0 / (1.0 + jnp.exp(-x))

    def coeffs(w, qs):
        inv = 1.0 / jnp.maximum(w, 1.0)
        temp = base + 0.5 * jnp.tanh(qs[2] * inv)
        rate = jnp.exp(2.0 * (1.0 - 1.0 / temp))
        return temp, rate, 0.2 * sigmoid(qs[1] * inv), 0.3 * sigmoid(qs[0] * inv), 0.2 * sigmoid(qs[3] * inv)

    def line(x, k):
        return x[k:k + 1, :]

    temp, rate, mixing, carried, loss = coeffs(line(total, 0), [line(total, 1 + k) for k in range(4)])
    _, ratep, mixingp, carriedp, _ = coeffs(
        line(before_sums, 0), [line(before_sums, 1 + k) for k in range(4)])
    up0 = cur + mixing * lap_c - carried * (cur - prev) + 0.2 * (rc * rate)
    pp0 = prev + mixingp * lap_p - carriedp * (prev - prev2) + 0.2 * (rp * ratep)
    pp0 = jnp.where(s >= 1, pp0, 0.0)
    rup = rc + mixing * lap_rc - carried * (rc - rp) + 0.2 * (rate * rrc)
    rho0 = 1.0 / (temp * (1.0 + jnp.sum(wcol * up0 * up0, axis=0, keepdims=True) / K))
    tc0 = temp + 0.1 * (rate * frc) - loss * (temp - 0.5)

    count = line(total, 5)
    fs = [line(total, 6 + k) for k in range(4)]
    fs[2] = 0.7 * fs[2] + 0.3 * (tc0 * count)
    temp, rate, mixing, carried, loss = coeffs(rho0 * count, [rho0 * x for x in fs])
    react = rup * rate
    up1 = up0 + mixing * lap_bins(up0) - carried * (up0 - pp0) + 0.2 * react
    sp_out[0] = up1
    rho1 = 1.0 / (temp * (1.0 + jnp.sum(wcol * up1 * up1, axis=0, keepdims=True) / K))
    tc1 = temp + 0.1 * jnp.sum(fcol * react, axis=0, keepdims=True) - loss * (temp - 0.5)

    table[s, 0:1, :] = rho1
    table[s, 1:2, :] = tc0
    table[s, 2:3, :] = tc1

    mine = table.at[s, 0:ROWS]

    @pl.loop(1, N)
    def _(d):
        pltpu.make_async_remote_copy(
            mine, mine, tsend, trecv, device_id=dev(lax.rem(s + d, N)), device_id_type=MESH).start()

    pltpu.make_async_copy(in1, in1, send1s).wait()
    pltpu.make_async_copy(in2, in2, send2s).wait()
    outp.wait_send()
    some = table.at[0:N - 1, 0:ROWS]
    pltpu.make_async_copy(some, some, trecv).wait()

    for c in range(C):
        tabc[c * 8:c * 8 + ROWS, :] = table[owner[c], 0:ROWS, :]
    rho_col, t0_col, t1_col = (tabc[pl.ds(k, C, stride=8), :] for k in range(ROWS))

    def look(col, index):
        return jnp.take_along_axis(col, index, axis=1, mode="promise_in_bounds")

    def cells(col):
        return jnp.concatenate([look(col, bins[:, o:o + 128]) for o in range(0, Z, 128)], axis=1)

    den_out[...] = cells(rho_col)
    t0, t1 = cells(t0_col), cells(t1_col)
    t0_left = edge(look(t0_col, jnp.clip(from_left, 0.0, B - 1.0).astype(jnp.int32)), 8)
    t0_right = edge(look(t0_col, jnp.clip(from_right, 0.0, B - 1.0).astype(jnp.int32)), 8)
    a = ahead[2]
    a = a + 0.3 * (t0 - a)
    al, ar = ends[2]
    al = al + 0.3 * (t0_left - al)
    ar = ar + 0.3 * (t0_right - ar)
    down, up = shifted(a, al, ar)
    a = a + 0.2 * (down + up - 2.0 * a)
    f_out[2] = a + 0.3 * (t1 - a)
    pltpu.make_async_copy(some, some, tsend).wait()


def body(density, fields, bins, owner, species, rate_matrix, inv_weight, formation):
    n, J = lax.axis_size("sec"), lax.axis_size("span")
    C, Z = density.shape
    _, K, B = species.shape
    PK = max(1, 8 // J)
    G = -(-NQ // PK)
    T1 = G * PK * J
    vm = pl.BlockSpec(memory_space=pltpu.VMEM)
    sm = pl.BlockSpec(memory_space=pltpu.SMEM)
    dma = pltpu.SemaphoreType.DMA
    return pl.pallas_call(
        functools.partial(kernel, n, J, PK),
        out_shape=(
            jax.ShapeDtypeStruct(species.shape, F32),
            jax.ShapeDtypeStruct(density.shape, F32),
            jax.ShapeDtypeStruct(fields.shape, F32),
        ),
        in_specs=[sm, sm, sm, vm, vm, vm, vm, vm],
        out_specs=(vm, vm, vm),
        scratch_shapes=[
            pltpu.VMEM((2, C, 128), F32),
            pltpu.VMEM((2, C, 128), F32),
            pltpu.VMEM((2, K, B), F32),
            pltpu.VMEM((Z // 128, 16 * C, 128), F32),
            pltpu.VMEM((C * 16, B), F32),
            pltpu.VMEM((n, T1, B), F32),
            pltpu.VMEM((n - 1, T1, B), F32),
            pltpu.VMEM((T1, B), F32),
            pltpu.VMEM((J, 16, B), F32),
            pltpu.VMEM((J - 1, 16, B), F32),
            pltpu.VMEM((8, B), F32),
            pltpu.VMEM((J, 8, B), F32),
            pltpu.VMEM((8, B), F32),
            pltpu.VMEM((n * J, 8, B), F32),
            pltpu.VMEM((C * 8, B), F32),
            dma((2,)), dma((2,)), dma((2,)), dma((2,)),
            dma, dma, dma, dma, dma, dma, dma, dma,
        ],
        compiler_params=pltpu.CompilerParams(
            collective_id=0, has_side_effects=True, vmem_limit_bytes=32 * 2**20),
        name="coupling",
    )(owner, inv_weight, formation, density, fields, bins, species, rate_matrix)


def solution(mesh):
    return jax.shard_map(
        body,
        mesh=mesh,
        in_specs=(
            P("sec", "span"),
            P(None, "sec", "span"),
            P("sec", "span"),
            P("sec"),
            P(("sec", "span"), None, None),
            P(),
            P(),
            P(),
        ),
        out_specs=(P(("sec", "span"), None, None), P("sec", "span"), P(None, "sec", "span")),
        check_vma=False,
    )
```

```python
import functools

import jax
import jax.numpy as jnp
from jax import lax
from jax.experimental import pallas as pl
from jax.experimental.pallas import tpu as pltpu
from jax.sharding import PartitionSpec as P

MESH = pl.DeviceIdType.MESH
F32 = jnp.float32
BF16 = jnp.bfloat16
HIGH = lax.Precision.HIGHEST
NQ = 10
ROWS = 3


def split(x):
    hi = x.astype(BF16)
    return hi, (x - hi.astype(F32)).astype(BF16)


def iota(shape, dim):
    return lax.broadcasted_iota(jnp.int32, shape, dim)


def shifted(x, left, right):
    width = x.shape[1]
    lane = iota(x.shape, 1)
    down = jnp.where(lane == 0, left, pltpu.roll(x, 1, 1))
    up = jnp.where(lane == width - 1, right, pltpu.roll(x, width - 1, 1))
    return down, up


def lap_bins(x):
    down, up = shifted(x, 0.0, 0.0)
    return up + down - 2.0 * x


def kernel(
    n, J, PK,
    owner_h, invw_h, form_h, density_h, fields_h, bins_h, species_h, rate_h,
    sp_out, den_out, f_out,
    owner, invw, form, density, fields, bins, species, rate_m, loads,
    halo_out, halo_in, spin, vals, hist, send1, in1, sum1, send2, in2, sendp, inp, prevs,
    table, tabc,
    hsend, hrecv, ssend, srecv, send1s, recv1s, send2s, recv2s, sendps, recvps, tsend, trecv,
):
    C, Z = density.shape
    K, B = species.shape[1], species.shape[2]
    N = n * J
    i, j = lax.axis_index("sec"), lax.axis_index("span")
    s = i * J + j

    def wrap(x, size):
        return jnp.where(x >= size, x - size, x)

    def dev(t):
        return (lax.div(t, J), lax.rem(t, J))

    pairs = ((fields_h, fields), (bins_h, bins), (density_h, density), (owner_h, owner),
             (species_h, species), (rate_h, rate_m), (invw_h, invw), (form_h, form))
    reads = [pltpu.make_async_copy(a, b, loads.at[k]) for k, (a, b) in enumerate(pairs)]
    for c in reads:
        c.start()

    barrier = pltpu.get_barrier_semaphore()

    for d in range(1, n):
        pl.semaphore_signal(barrier, inc=1, device_id=(wrap(i + d, n), j), device_id_type=MESH)
    for d in range(1, J):
        pl.semaphore_signal(barrier, inc=1, device_id=(i, wrap(j + d, J)), device_id_type=MESH)

    reads[0].wait()
    reads[1].wait()
    lane = iota((C, 128), 1)
    binf = bins[...].astype(F32)
    first, last = binf[:, :128], binf[:, Z - 128:]
    to_left = jnp.where(lane == 8, pltpu.roll(first, 8, 1), 0.0)
    to_right = jnp.where(lane == 8, pltpu.roll(last, 9, 1), 0.0)
    for k in range(4):
        here = (lane == 2 * k) | (lane == 2 * k + 1)
        head, tail = fields[k, :, :128], fields[k, :, Z - 128:]
        if k:
            head = pltpu.roll(head, 2 * k, 1)
        to_left = jnp.where(here, head, to_left)
        to_right = jnp.where(here, pltpu.roll(tail, 2 * k + 2, 1), to_right)
    halo_out[0] = to_left
    halo_out[1] = to_right

    pl.semaphore_wait(barrier, n + J - 2)

    copies = []
    for side, step in ((0, J - 1), (1, 1)):
        copies.append(pltpu.make_async_remote_copy(
            halo_out.at[side], halo_in.at[side], hsend.at[side], hrecv.at[side],
            device_id=(i, wrap(j + step, J)), device_id_type=MESH))
    for step in (1, 2):
        copies.append(pltpu.make_async_remote_copy(
            species_h.at[0], spin.at[step - 1], ssend.at[step - 1], srecv.at[step - 1],
            device_id=dev(lax.rem(s + step, N)), device_id_type=MESH))
    for c in copies[:2]:
        c.start()
    for step in (1, 2):
        pl.when(j + step < J)(copies[1 + step].start)

    reads[2].wait()
    den = density[...]

    def put(k, x):
        for h in range(Z // 128):
            vals[h, k * C:(k + 1) * C, :] = x[:, h * 128:(h + 1) * 128]

    put(0, den)
    put(5, jnp.ones((C, Z), F32))
    for k in range(4):
        f = fields[k]
        put(1 + k, den * f)
        down, up = shifted(f, 0.0, 0.0)
        put(6 + k, f + 0.2 * (down + up - 2.0 * f))
    for k in range(NQ, 16):
        put(k, jnp.zeros((C, Z), F32))

    bin_id = iota((B, Z), 0)
    for c in range(C):
        hot = jnp.where(bin_id == bins[c:c + 1, :], 1.0, 0.0).astype(BF16)
        v = jnp.concatenate([vals[h, pl.ds(c, 16, stride=C), :] for h in range(Z // 128)], axis=1)
        hi, lo = split(v)
        both = jnp.concatenate([hi, lo], axis=0)
        r = lax.dot_general(both, hot, (((1,), (1,)), ((), ())), preferred_element_type=F32)
        hist[c * 16:(c + 1) * 16, :] = r[:16] + r[16:]

    RT = PK * J
    R, PC = n * RT, PK * C
    G = -(-NQ // PK)
    reads[3].wait()
    q = iota((1, PC), 1)
    qc = lax.rem(q, C)
    own_lane = jnp.zeros((1, PC), jnp.int32)
    for c in range(C):
        own_lane = jnp.where(qc == c, owner[c], own_lane)
    r = iota((R, PC), 0)
    rem = lax.rem(r, RT)
    sec = lax.div(r, RT) * J + lax.rem(rem, J)
    same = lax.div(rem, J) == lax.div(iota((R, PC), 1), C)
    place = jnp.where(same & (sec == own_lane), 1.0, 0.0).astype(BF16)

    for c in copies[:2]:
        c.wait()
    from_left, from_right = halo_in[1], halo_in[0]
    lanes_b = iota((C, B), 1)
    bin_first, bin_last = bins[:, 0:1], bins[:, Z - 1:Z]
    hot_first = jnp.where(lanes_b == bin_first, 0.2, 0.0)
    hot_last = jnp.where(lanes_b == bin_last, 0.2, 0.0)

    def edge(tile, at):
        return tile[:, at:at + 1]

    slabs = []
    for k in range(G * PK):
        h = hist[pl.ds(k, C, stride=16), :]
        if 6 <= k < NQ:
            h = (h + hot_first * edge(from_left, 2 * (k - 6) + 1)
                 + hot_last * edge(from_right, 2 * (k - 6)))
        slabs.append(h)
    groups = []
    for g in range(G):
        part = slabs[g * PK:(g + 1) * PK]
        groups.append(part[0] if PK == 1 else jnp.concatenate(part, axis=0))
    wide = jnp.concatenate(groups, axis=1)
    hi, lo = split(wide)
    binned = (jnp.dot(place, hi, preferred_element_type=F32)
              + jnp.dot(place, lo, preferred_element_type=F32))
    for t in range(n):
        for g in range(G):
            send1[t, g * RT:(g + 1) * RT, :] = binned[t * RT:(t + 1) * RT, g * 128:(g + 1) * 128]

    outs1 = []
    for d in range(1, n):
        t = wrap(i + d, n)
        outs1.append(pltpu.make_async_remote_copy(
            send1.at[t], in1.at[d - 1], send1s, recv1s, device_id=(t, j), device_id_type=MESH))
    for c in outs1:
        c.start()

    for c in reads[4:]:
        c.wait()
    row = iota((K, B), 0)
    wcol = jnp.zeros((K, B), F32)
    fcol = jnp.zeros((K, B), F32)
    for k in range(K):
        wcol = jnp.where(row == k, invw[k], wcol)
        fcol = jnp.where(row == k, form[k], fcol)
    cur = species[0]
    rm = rate_m[...]
    rc = jnp.dot(rm, cur, precision=HIGH, preferred_element_type=F32)
    rrc = jnp.dot(rm, rc, precision=HIGH, preferred_element_type=F32)
    lap_c, lap_rc = lap_bins(cur), lap_bins(rc)
    frc = jnp.sum(fcol * rc, axis=0, keepdims=True)

    lane256 = iota((C, Z), 1)
    ahead = []
    ends = []
    for k in range(4):
        f = fields[k]
        l2, l1 = edge(from_left, 2 * k), edge(from_left, 2 * k + 1)
        r1, r2 = edge(from_right, 2 * k), edge(from_right, 2 * k + 1)
        down, up = shifted(f, l1, r1)
        a = f + 0.2 * (down + up - 2.0 * f)
        al = l1 + 0.2 * (l2 + f[:, 0:1] - 2.0 * l1)
        ar = r1 + 0.2 * (r2 + f[:, Z - 1:Z] - 2.0 * r1)
        ahead.append(a)
        ends.append((al, ar))
        if k != 2:
            down, up = shifted(a, al, ar)
            f_out[k] = a + 0.2 * (down + up - 2.0 * a)

    pltpu.make_async_copy(in1, in1, recv1s).wait()
    total = send1[i]
    for d in range(n - 1):
        total = total + in1[d]
    sum1[...] = total
    for t in range(J):
        send2[t, 0:NQ, :] = sum1[pl.ds(t, NQ, stride=J), :]
        if t:
            send2[t, NQ:NQ + 5, :] = sum1[pl.ds(t - 1, 5, stride=J), :]
        else:
            send2[t, NQ:NQ + 5, :] = jnp.zeros((5, B), F32)
        send2[t, NQ + 5:16, :] = jnp.zeros((1, B), F32)
    sendp[0:5, :] = sum1[pl.ds(J - 1, 5, stride=J), :]
    sendp[5:8, :] = jnp.zeros((3, B), F32)
    outp = pltpu.make_async_remote_copy(
        sendp, inp.at[j], sendps, recvps, device_id=(wrap(i + 1, n), 0), device_id_type=MESH)
    outs2 = []
    for d in range(1, J):
        t = wrap(j + d, J)
        outs2.append(pltpu.make_async_remote_copy(
            send2.at[t], in2.at[d - 1], send2s, recv2s, device_id=(i, t), device_id_type=MESH))
    outp.start()
    for c in outs2:
        c.start()

    for step in (1, 2):
        pl.when(j + step >= J)(copies[1 + step].start)
    for c in copies[2:]:
        c.wait()
    prev = jnp.where(s >= 1, spin[0], 0.0)
    prev2 = jnp.where(s >= 2, spin[1], 0.0)
    rp = jnp.dot(rm, prev, precision=HIGH, preferred_element_type=F32)
    lap_p = lap_bins(prev)

    pltpu.make_async_copy(in2, in2, recv2s).wait()
    total = send2[j]
    for d in range(J - 1):
        total = total + in2[d]
    prevs[0:5, :] = total[NQ:NQ + 5]

    @pl.when(j == 0)
    def _():
        pltpu.make_async_copy(inp, inp, recvps).wait()
        tp = inp[0]
        for d in range(1, J):
            tp = tp + inp[d]
        prevs[...] = tp

    before_sums = prevs[...]
    eta = (iota((1, B), 1).astype(F32) + 0.5) / B
    base = 1.0 + 4.0 * eta * (1.0 - eta)

    def sigmoid(x):
        return 1.0 / (1.0 + jnp.exp(-x))

    def coeffs(w, qs):
        inv = 1.0 / jnp.maximum(w, 1.0)
        temp = base + 0.5 * jnp.tanh(qs[2] * inv)
        rate = jnp.exp(2.0 * (1.0 - 1.0 / temp))
        return temp, rate, 0.2 * sigmoid(qs[1] * inv), 0.3 * sigmoid(qs[0] * inv), 0.2 * sigmoid(qs[3] * inv)

    def line(x, k):
        return x[k:k + 1, :]

    temp, rate, mixing, carried, loss = coeffs(line(total, 0), [line(total, 1 + k) for k in range(4)])
    _, ratep, mixingp, carriedp, _ = coeffs(
        line(before_sums, 0), [line(before_sums, 1 + k) for k in range(4)])
    up0 = cur + mixing * lap_c - carried * (cur - prev) + 0.2 * (rc * rate)
    pp0 = prev + mixingp * lap_p - carriedp * (prev - prev2) + 0.2 * (rp * ratep)
    pp0 = jnp.where(s >= 1, pp0, 0.0)
    rup = rc + mixing * lap_rc - carried * (rc - rp) + 0.2 * (rate * rrc)
    rho0 = 1.0 / (temp * (1.0 + jnp.sum(wcol * up0 * up0, axis=0, keepdims=True) / K))
    tc0 = temp + 0.1 * (rate * frc) - loss * (temp - 0.5)

    count = line(total, 5)
    fs = [line(total, 6 + k) for k in range(4)]
    fs[2] = 0.7 * fs[2] + 0.3 * (tc0 * count)
    temp, rate, mixing, carried, loss = coeffs(rho0 * count, [rho0 * x for x in fs])
    react = rup * rate
    up1 = up0 + mixing * lap_bins(up0) - carried * (up0 - pp0) + 0.2 * react
    sp_out[0] = up1
    rho1 = 1.0 / (temp * (1.0 + jnp.sum(wcol * up1 * up1, axis=0, keepdims=True) / K))
    tc1 = temp + 0.1 * jnp.sum(fcol * react, axis=0, keepdims=True) - loss * (temp - 0.5)

    table[s, 0:1, :] = rho1
    table[s, 1:2, :] = tc0
    table[s, 2:3, :] = tc1

    mine = table.at[s, 0:ROWS]

    def tell(d, first):
        for e in range(first, J):
            pltpu.make_async_remote_copy(
                mine, mine, tsend, trecv, device_id=(wrap(i + d, n), wrap(j + e, J)),
                device_id_type=MESH).start()

    tell(0, 1)
    if N <= 64:
        for d in range(1, n):
            tell(d, 0)
    else:
        pl.loop(1, n)(lambda d: tell(d, 0))

    pltpu.make_async_copy(in1, in1, send1s).wait()
    pltpu.make_async_copy(in2, in2, send2s).wait()
    outp.wait_send()
    some = table.at[0:N - 1, 0:ROWS]
    pltpu.make_async_copy(some, some, trecv).wait()

    for c in range(C):
        tabc[c * 8:c * 8 + ROWS, :] = table[owner[c], 0:ROWS, :]
    rho_col, t0_col, t1_col = (tabc[pl.ds(k, C, stride=8), :] for k in range(ROWS))

    def look(col, index):
        return jnp.take_along_axis(col, index, axis=1, mode="promise_in_bounds")

    def cells(col):
        return jnp.concatenate([look(col, bins[:, o:o + 128]) for o in range(0, Z, 128)], axis=1)

    den_out[...] = cells(rho_col)
    t0, t1 = cells(t0_col), cells(t1_col)
    t0_left = edge(look(t0_col, jnp.clip(from_left, 0.0, B - 1.0).astype(jnp.int32)), 8)
    t0_right = edge(look(t0_col, jnp.clip(from_right, 0.0, B - 1.0).astype(jnp.int32)), 8)
    a = ahead[2]
    a = a + 0.3 * (t0 - a)
    al, ar = ends[2]
    al = al + 0.3 * (t0_left - al)
    ar = ar + 0.3 * (t0_right - ar)
    down, up = shifted(a, al, ar)
    a = a + 0.2 * (down + up - 2.0 * a)
    f_out[2] = a + 0.3 * (t1 - a)
    pltpu.make_async_copy(some, some, tsend).wait()


def store(a, b, c, a_out, b_out, c_out, sems):
    copies = [pltpu.make_async_copy(x, y, sems.at[k])
              for k, (x, y) in enumerate(((a, a_out), (b, b_out), (c, c_out)))]
    for x in copies:
        x.start()
    for x in copies:
        x.wait()


def body(density, fields, bins, owner, species, rate_matrix, inv_weight, formation):
    n, J = lax.axis_size("sec"), lax.axis_size("span")
    C, Z = density.shape
    _, K, B = species.shape
    PK = max(1, 8 // J)
    G = -(-NQ // PK)
    T1 = G * PK * J
    vm = pl.BlockSpec(memory_space=pltpu.VMEM)
    hbm = pl.BlockSpec(memory_space=pltpu.HBM)
    dma = pltpu.SemaphoreType.DMA
    results = pl.pallas_call(
        functools.partial(kernel, n, J, PK),
        out_shape=(
            jax.ShapeDtypeStruct(species.shape, F32),
            jax.ShapeDtypeStruct(density.shape, F32),
            jax.ShapeDtypeStruct(fields.shape, F32),
        ),
        in_specs=[hbm] * 8,
        out_specs=(vm, vm, vm),
        scratch_shapes=[
            pltpu.SMEM(owner.shape, jnp.int32),
            pltpu.SMEM(inv_weight.shape, F32),
            pltpu.SMEM(formation.shape, F32),
            pltpu.VMEM(density.shape, F32),
            pltpu.VMEM(fields.shape, F32),
            pltpu.VMEM(bins.shape, jnp.int32),
            pltpu.VMEM(species.shape, F32),
            pltpu.VMEM(rate_matrix.shape, F32),
            dma((8,)),
            pltpu.VMEM((2, C, 128), F32),
            pltpu.VMEM((2, C, 128), F32),
            pltpu.VMEM((2, K, B), F32),
            pltpu.VMEM((Z // 128, 16 * C, 128), F32),
            pltpu.VMEM((C * 16, B), F32),
            pltpu.VMEM((n, T1, B), F32),
            pltpu.VMEM((n - 1, T1, B), F32),
            pltpu.VMEM((T1, B), F32),
            pltpu.VMEM((J, 16, B), F32),
            pltpu.VMEM((J - 1, 16, B), F32),
            pltpu.VMEM((8, B), F32),
            pltpu.VMEM((J, 8, B), F32),
            pltpu.VMEM((8, B), F32),
            pltpu.VMEM((n * J, 8, B), F32),
            pltpu.VMEM((C * 8, B), F32),
            dma((2,)), dma((2,)), dma((2,)), dma((2,)),
            dma, dma, dma, dma, dma, dma, dma, dma,
        ],
        compiler_params=pltpu.CompilerParams(
            collective_id=0, has_side_effects=True),
        name="coupling",
    )(owner, inv_weight, formation, density, fields, bins, species, rate_matrix)
    return pl.pallas_call(
        store,
        out_shape=tuple(jax.ShapeDtypeStruct(r.shape, F32) for r in results),
        in_specs=[vm] * 3,
        out_specs=(hbm,) * 3,
        scratch_shapes=[dma((3,))],
        name="store",
    )(*results)


def solution(mesh):
    return jax.shard_map(
        body,
        mesh=mesh,
        in_specs=(
            P("sec", "span"),
            P(None, "sec", "span"),
            P("sec", "span"),
            P("sec"),
            P(("sec", "span"), None, None),
            P(),
            P(),
            P(),
        ),
        out_specs=(P(("sec", "span"), None, None), P("sec", "span"), P(None, "sec", "span")),
        check_vma=False,
    )
```
